32 devices in a mesh: tm: 16 (over z, y, core), chan: 2 (over x).
Axes of the slice: x: 2, y: 2, z: 4, core: 2. Of those that a mesh axis runs over, the one named last changes fastest.
Arguments:
- clip_input: bfloat16 [512, 32, 256], P('chan', 'tm'), may hold values from -16 to 16, as said below
- lengths: int32 [8], replicated, may hold values from 1 to 16, 32 in all
- gamma_one: float32 [512], P('chan'), may hold values from 0.25 to 1.75
- beta_one: float32 [512], P('chan'), may hold values from -1.5 to 1.5
- w_one: bfloat16 [512, 27, 512], P('chan'), may hold values from -0.0546875 to 0.0546875
- bias_one: float32 [512], P('chan'), may hold values from -1.5 to 1.5
- gamma_two: float32 [512], P('chan'), may hold values from 0.25 to 1.75
- beta_two: float32 [512], P('chan'), may hold values from -1.5 to 1.5
- w_two: bfloat16 [512, 27, 512], P('chan'), may hold values from -0.0546875 to 0.0546875
- bias_two: float32 [512], P('chan'), may hold values from -1.5 to 1.5
Outputs:
- block_output: float32 [512, 32, 256], P('chan', 'tm')
The draws below stay inside these ranges and needn't reach their ends.
Inputs may be any that keep to these rules, and one draw needn't show every extreme that they name: `clip_input`: activations of order one. `lengths`: the 8 counts sum to 32; the longest is exactly 16.
All inputs are finite; a program needn't handle non-finite values.
Results may differ from the reference program's by a relative error of at most 0.0054.
Values may be sent and summed in bfloat16 or wider, within the bound.
A program may use at most 128 MiB of HBM per device.

```python
import math
import jax
import jax.numpy as jnp
import numpy as np
from jax import lax

C = 512
GROUPS = 32
H = 16
W = 16
FRAMES = 32
NCLIP = 8
MOST = 16


def draw_clip_input(key, part):
    k_base, k_chan, k_frame = jax.random.split(key, 3)
    chan_scale = jnp.exp(jax.random.uniform(k_chan, (C, 1, 1), jnp.float32, math.log(0.5), math.log(2.0)))
    frame_scale = jnp.exp(jax.random.uniform(k_frame, (1, FRAMES, 1), jnp.float32, math.log(0.5), math.log(2.0)))
    base = jnp.clip(jax.random.normal(k_base, (C, FRAMES, H * W), jnp.float32), -4.0, 4.0)
    return (base * chan_scale * frame_scale).astype(jnp.bfloat16)


def block_levels(stream_key, shape, cuts, low, high):
    factor_of = 1.0
    for dim, parts in cuts:
        steps = jax.random.uniform(jax.random.fold_in(jax.random.fold_in(stream_key, 6), dim), (parts,), jnp.float32, low / len(cuts), high / len(cuts))
        factor_of = factor_of * jnp.repeat(jnp.exp(steps), shape[dim] // parts).reshape((-1,) + (1,) * (len(shape) - 1 - dim))
    return factor_of


def profile(number_of, total, limit, skew):
    weights = [(1 << 20) // math.isqrt(standing ** skew) + 1 for standing in range(2, number_of + 1)]
    surplus, given = total - limit - (number_of - 1), [1] * (number_of - 1)
    while surplus > 0:
        candidates = [i for i in range(number_of - 1) if given[i] < limit]
        whole, budget = sum([weights[i] for i in candidates]), surplus
        for i in candidates:
            extra = min(limit - given[i], max(1, budget * weights[i] // whole), surplus)
            given[i] = given[i] + extra
            surplus = surplus - extra
    return np.array([limit] + given)


def ragged(own_key, amount, total, reach, lean):
    if amount == 2:
        one = jax.random.randint(own_key, (), max(1, total - reach), min(reach, total - 1) + 1)
        return jnp.stack([one, total - one])
    sizes = jnp.asarray(profile(amount, total, reach, lean), jnp.int32)
    twos = (amount - 1) // 2
    source_of, sink = sizes[1:1 + 2 * twos:2], sizes[2:2 + 2 * twos:2]
    slack = jnp.minimum(source_of - 1, reach - sink)
    moved = jax.random.randint(jax.random.fold_in(own_key, 1), (twos,), 0, 1 << 20) % (slack + 1)
    sizes = sizes.at[1:1 + 2 * twos:2].set(source_of - moved).at[2:2 + 2 * twos:2].set(sink + moved)
    return sizes[jax.random.permutation(jax.random.fold_in(own_key, 2), amount)]


def centred(key, extent, width, limit, cuts=(), held_as=jnp.bfloat16):
    level = block_levels(key, extent, cuts, -0.22, 0.18) if cuts else 1.0
    entries = jax.random.normal(key, extent, jnp.float32) * width * level
    return jnp.minimum(jnp.maximum(entries, -limit), limit).astype(held_as)


def setup_inputs(seed: int = 0) -> dict:
    keys = jax.random.split(jax.random.key(seed), 11)
    clip_input = draw_clip_input(jax.random.fold_in(keys[10], 71), 0)
    lengths = ragged(keys[1], NCLIP, FRAMES, MOST, 2).astype(jnp.int32)
    gamma_one = jnp.clip(1.0 + 0.15 * jax.random.normal(keys[2], (C,), jnp.float32), 0.25, 1.75)
    beta_one = centred(keys[3], (C,), 0.3, 1.5, ((0, 2),), jnp.float32)
    w_one = centred(keys[4], (C, 27, C), (27 * C) ** -0.5, 0.0546875, ((0, 2),))
    bias_one = centred(keys[5], (C,), 0.3, 1.5, ((0, 2),), jnp.float32)
    gamma_two = jnp.clip(1.0 + 0.15 * jax.random.normal(keys[6], (C,), jnp.float32), 0.25, 1.75)
    beta_two = centred(keys[7], (C,), 0.3, 1.5, ((0, 2),), jnp.float32)
    w_two = centred(keys[8], (C, 27, C), (27 * C) ** -0.5, 0.0546875, ((0, 2),))
    bias_two = centred(keys[9], (C,), 0.3, 1.5, ((0, 2),), jnp.float32)
    return {"clip_input": clip_input, "lengths": lengths, "gamma_one": gamma_one, "beta_one": beta_one, "w_one": w_one, "bias_one": bias_one, "gamma_two": gamma_two, "beta_two": beta_two, "w_two": w_two, "bias_two": bias_two}


EPS = 1e-06

def clip_of(frames, ends):
    return lax.optimization_barrier(jnp.sum((frames[:, None] >= ends[None, :]).astype(jnp.int32), axis=1)).astype(jnp.int32)

def group_norm(data, gamma, beta, member, counts):
    chans, frames, cells = data.shape
    grouped = data.reshape(GROUPS, chans // GROUPS, frames, cells)
    sums = lax.optimization_barrier(jnp.sum(grouped, axis=(1, 3)))
    squares = lax.optimization_barrier(jnp.sum(grouped * grouped, axis=(1, 3)))
    clip_sum = jnp.dot(sums, member, precision=lax.Precision.HIGHEST)
    clip_sq = jnp.dot(squares, member, precision=lax.Precision.HIGHEST)
    mean = clip_sum / counts[None, :]
    var = clip_sq / counts[None, :] - mean * mean
    scale = lax.rsqrt(var + EPS)
    mean_f = jnp.dot(mean, member.T, precision=lax.Precision.HIGHEST)
    scale_f = jnp.dot(scale, member.T, precision=lax.Precision.HIGHEST)
    normed = (grouped - mean_f[:, None, :, None]) * scale_f[:, None, :, None]
    normed = normed.reshape(chans, frames, cells) * gamma[:, None, None] + beta[:, None, None]
    return jax.nn.silu(normed).astype(jnp.bfloat16)

def causal_conv(hidden, weight, bias, ends, starts):
    chans, frames, cells = hidden.shape
    padded = jnp.pad(hidden.reshape(chans, frames, H, W), ((0, 0), (0, 0), (1, 1), (1, 1)))
    flat_w = weight.reshape(chans * 27, weight.shape[2])

    def one_frame(g):
        clip = clip_of(g[None], ends)[0]
        first = starts[clip]
        pieces = []
        for kt in range(3):
            src = g - 2 + kt
            keep = (src >= first).astype(jnp.bfloat16)
            frame = lax.dynamic_index_in_dim(padded, jnp.maximum(src, 0).astype(jnp.int32), 1, keepdims=False) * keep
            for kh in range(3):
                for kw in range(3):
                    pieces.append(frame[:, kh:kh + H, kw:kw + W].reshape(chans, H * W))
        cols = jnp.stack(pieces, axis=1).reshape(chans * 27, H * W)
        return jnp.dot(flat_w.T, cols, preferred_element_type=jnp.float32)
    out = lax.map(one_frame, jnp.arange(frames, dtype=jnp.int32))
    return jnp.transpose(out, (1, 0, 2)) + bias[:, None, None]

def reference(clip_input, lengths, gamma_one, beta_one, w_one, bias_one, gamma_two, beta_two, w_two, bias_two):
    ends = jnp.cumsum(lengths).astype(jnp.int32)
    starts = (ends - lengths).astype(jnp.int32)
    clips = clip_of(jnp.arange(FRAMES, dtype=jnp.int32), ends)
    member = (clips[:, None] == jnp.arange(NCLIP, dtype=jnp.int32)[None, :]).astype(jnp.float32)
    counts = lengths.astype(jnp.float32) * float(C // GROUPS * H * W)
    data = clip_input.astype(jnp.float32)
    h_one = group_norm(data, gamma_one, beta_one, member, counts)
    y_one = causal_conv(h_one, w_one, bias_one, ends, starts).astype(jnp.bfloat16)
    h_two = group_norm(y_one.astype(jnp.float32), gamma_two, beta_two, member, counts)
    y_two = causal_conv(h_two, w_two, bias_two, ends, starts)
    return data + y_two
```

```python
import functools

import jax
import jax.numpy as jnp
from jax import lax
from jax.experimental import pallas as pl
from jax.experimental.pallas import tpu as pltpu
from jax.sharding import PartitionSpec as P

C = 512
GROUPS = 32
SIZE = C // GROUPS
H = 16
W = 16
CELLS = H * W
PAD = CELLS + 2 * W
EPS = 1e-06
MESH = pl.DeviceIdType.MESH
HIGHEST = lax.Precision.HIGHEST


def iota(shape, dim):
    return lax.broadcasted_iota(jnp.int32, shape, dim)


def dot(a, b, precision=None):
    return lax.dot_general(
        a, b, (((1,), (0,)), ((), ())), precision=precision, preferred_element_type=jnp.float32
    )


def kernel(
    n, T, nclip, wide,
    len_ref, x_ref, par_ref, w1_ref, w2_ref, out_ref,
    wbuf, hs, halo, stats, psend, precv, y_ref,
    w_sem, hsend, hrecv, ssend, srecv, qsend, qrecv,
):
    ci = x_ref.shape[1]
    me = lax.axis_index("tm")
    ch = lax.axis_index("chan")
    rows = 2 * CELLS

    def peer(d):
        return lax.rem(me + d, T), ch

    def partner(k):
        return me, lax.rem(ch + k, n)

    def w_copy(layer, k, part):
        w_ref = (w1_ref, w2_ref)[layer]
        tgt = lax.rem(ch + k, n)
        taps = pl.ds(9 * part, 9)
        if wide:
            src = w_ref.at[taps, :, pl.ds(pl.multiple_of(tgt * ci, ci), ci)]
        else:
            src = w_ref.at[tgt, taps]
        return pltpu.make_async_copy(src, wbuf.at[layer, k, taps], w_sem.at[layer, k, part])

    order = list(range(1, n)) + [0]
    for layer in range(2):
        for k in order:
            for part in (2, 1, 0):
                w_copy(layer, k, part).start()

    barrier = pltpu.get_barrier_semaphore()

    def greet(d, carry):
        pl.semaphore_signal(barrier, inc=1, device_id=peer(d), device_id_type=MESH)
        return carry

    lax.fori_loop(1, T, greet, 0)
    for k in range(1, n):
        pl.semaphore_signal(barrier, inc=1, device_id=partner(k), device_id_type=MESH)

    hs[:, :, :, 0:W, :] = jnp.zeros((3, 3, 2, W, ci), jnp.bfloat16)
    hs[:, :, :, W + CELLS :, :] = jnp.zeros((3, 3, 2, W, ci), jnp.bfloat16)

    @pl.when(me == 0)
    def _():
        halo[...] = jnp.zeros_like(halo)

    first = 2 * me
    starts, counts, spans = [], [], []
    for f in range(4):
        g = first - 2 + f
        begin = jnp.int32(0)
        count = jnp.int32(0)
        run = jnp.int32(0)
        for c in range(nclip):
            size = len_ref[c]
            inside = jnp.logical_and(run <= g, g < run + size)
            begin = jnp.where(inside, run, begin)
            count = jnp.where(inside, size, count)
            run = run + size
        starts.append(begin)
        counts.append(count)
        spans.append((begin, begin + count))

    def halo_copy(layer):
        src = x_ref if layer == 0 else y_ref
        return pltpu.make_async_remote_copy(
            src_ref=src, dst_ref=halo.at[layer],
            send_sem=hsend.at[layer], recv_sem=hrecv.at[layer],
            device_id=peer(1), device_id_type=MESH,
        )

    def stat_copy(layer, d):
        return pltpu.make_async_remote_copy(
            src_ref=stats.at[layer, me], dst_ref=stats.at[layer, me],
            send_sem=ssend.at[layer, d], recv_sem=srecv.at[layer, d],
            device_id=peer(d), device_id_type=MESH,
        )

    def part_copy(layer, k):
        return pltpu.make_async_remote_copy(
            src_ref=psend.at[layer, k - 1], dst_ref=precv.at[layer, k - 1],
            send_sem=qsend.at[layer, k - 1], recv_sem=qrecv.at[layer, k - 1],
            device_id=partner(k), device_id_type=MESH,
        )

    lane_group = (iota((ci, 128), 1) % 32 == iota((ci, 128), 0) // SIZE).astype(jnp.float32)
    lane_t = iota((128, ci), 0)
    member = lane_t % 32 == iota((128, ci), 1) // SIZE
    pick_sum = jnp.logical_and(member, lane_t < 64).astype(jnp.float32)
    pick_sq = jnp.logical_and(member, lane_t >= 64).astype(jnp.float32)

    def local_stats(layer, a, b):
        lines = [
            jnp.sum(v, axis=0, keepdims=True) for v in (a, b, a * a, b * b)
        ] + [jnp.zeros((4, ci), jnp.float32)]
        by_group = dot(jnp.concatenate(lines, axis=0), lane_group, HIGHEST)
        own = iota((8, 128), 0) == iota((8, 128), 1) // 32
        stats[layer, me] = jnp.sum(jnp.where(own, by_group, 0.0), axis=0, keepdims=True)

    def send_stats(layer):
        def go(d, carry):
            stat_copy(layer, d).start()
            return carry

        lax.fori_loop(1, T, go, 0)

    def clip_stats(layer):
        def come(d, carry):
            stat_copy(layer, d).wait_recv()
            return carry

        lax.fori_loop(1, T, come, 0)
        every = stats[layer]
        frame = 2 * iota((T, 1, 128), 0) + (iota((T, 1, 128), 2) // 32) % 2
        lines = []
        for f in range(4):
            low, high = spans[f]
            inside = jnp.logical_and(frame >= low, frame < high)
            total = jnp.sum(jnp.where(inside, every, 0.0), axis=0)
            cells = jnp.maximum(counts[f], 1).astype(jnp.float32) * float(SIZE * CELLS)
            lines.append(total / jnp.full((1, 128), cells))
        lines = jnp.concatenate(lines + [jnp.zeros((4, 128), jnp.float32)], axis=0)
        mean = dot(lines, pick_sum, HIGHEST)
        var = dot(lines, pick_sq, HIGHEST) - mean * mean
        return mean, lax.rsqrt(var + EPS)

    column = iota((CELLS, ci), 0) % W

    def place(layer, f, data, mean, scale, slots):
        gamma = par_ref[3 * layer : 3 * layer + 1, :]
        beta = par_ref[3 * layer + 1 : 3 * layer + 2, :]
        u = (data - mean[f : f + 1]) * (scale[f : f + 1] * gamma) + beta
        h = 0.5 * u * (1.0 + jnp.tanh(0.5 * u))
        before = jnp.where(column == 0, 0.0, pltpu.roll(h, 1, 0))
        after = jnp.where(column == W - 1, 0.0, pltpu.roll(h, CELLS - 1, 0))
        for kw, v in enumerate((before, h, after)):
            for kt, j in slots:
                if kt == 2:
                    kept = v
                else:
                    keep = jnp.full((CELLS, ci), starts[2 + j]) <= first + (j - 2 + kt)
                    kept = jnp.where(keep, v, 0.0)
                hs[kw, kt, j, W : W + CELLS, :] = kept.astype(jnp.bfloat16)

    def taps(layer, k, kt):
        w_copy(layer, k, kt).wait()
        if ci % 128 == 0:
            pieces = [
                hs[kw, kt, :, kh * W : kh * W + CELLS, :].reshape(rows, ci)
                for kh in range(3)
                for kw in range(3)
            ]
            weights = wbuf[layer, k, 9 * kt : 9 * kt + 9].reshape(9 * ci, ci)
            return dot(jnp.concatenate(pieces, axis=1), weights)
        total = None
        for kh in range(3):
            for kw in range(3):
                piece = hs[kw, kt, :, kh * W : kh * W + CELLS, :].reshape(rows, ci)
                term = dot(piece, wbuf[layer, k, 9 * kt + 3 * kh + kw])
                total = term if total is None else total + term
        return total

    def convolve(layer, a, b):
        local_stats(layer, a, b)
        send_stats(layer)
        mean, scale = clip_stats(layer)
        place(layer, 2, a, mean, scale, [(2, 0), (1, 1)])
        place(layer, 3, b, mean, scale, [(2, 1)])
        own = None
        for k in order:
            total = taps(layer, k, 2)
            if k == order[0]:

                @pl.when(me > 0)
                def _():
                    halo_copy(layer).wait_recv()

                place(layer, 0, halo[layer, 0:CELLS, :].astype(jnp.float32), mean, scale, [(0, 0)])
                place(
                    layer, 1, halo[layer, CELLS:, :].astype(jnp.float32), mean, scale,
                    [(1, 0), (0, 1)],
                )
            total = total + taps(layer, k, 1) + taps(layer, k, 0)
            if k:
                psend[layer, k - 1] = total.astype(jnp.bfloat16)
                part_copy(layer, k).start()
            else:
                own = total
        own = own + par_ref[3 * layer + 2 : 3 * layer + 3, :]
        for k in range(1, n):
            part_copy(layer, k).wait_recv()
            own = own + precv[layer, k - 1].astype(jnp.float32)
        return own

    pl.semaphore_wait(barrier, T - 1 + n - 1)

    @pl.when(me < T - 1)
    def _():
        halo_copy(0).start()

    x = x_ref[...].astype(jnp.float32)
    y_ref[...] = convolve(0, x[:CELLS], x[CELLS:]).astype(jnp.bfloat16)

    @pl.when(me < T - 1)
    def _():
        halo_copy(1).start()

    y = y_ref[...].astype(jnp.float32)
    z = convolve(1, y[:CELLS], y[CELLS:])
    out_ref[...] = x_ref[...].astype(jnp.float32) + z

    for layer in range(2):

        @pl.when(me < T - 1)
        def _():
            halo_copy(layer).wait_send()

        def sent(d, carry):
            stat_copy(layer, d).wait_send()
            return carry

        lax.fori_loop(1, T, sent, 0)
        for k in range(1, n):
            part_copy(layer, k).wait_send()


def on_device(n, T, x, lengths, g1, b1, w1, c1, g2, b2, w2, c2):
    ci, frames, cells = x.shape
    rows = frames * cells
    wide = ci % 128 == 0
    if wide:
        w1, w2 = [w.transpose(1, 0, 2) for w in (w1, w2)]
    else:
        w1, w2 = [w.reshape(ci, 27, n, ci).transpose(2, 1, 0, 3) for w in (w1, w2)]
    zero = jnp.zeros_like(g1)
    par = jnp.stack([g1, b1, c1, g2, b2, c2, zero, zero])
    xt = x.transpose(1, 2, 0).reshape(rows, ci)
    vmem = pl.BlockSpec(memory_space=pltpu.VMEM)
    hbm = pl.BlockSpec(memory_space=pl.ANY)
    dma = pltpu.SemaphoreType.DMA
    out = pl.pallas_call(
        functools.partial(kernel, n, T, lengths.shape[0], wide),
        out_shape=jax.ShapeDtypeStruct((rows, ci), jnp.float32),
        in_specs=[pl.BlockSpec(memory_space=pltpu.SMEM), vmem, vmem, hbm, hbm],
        out_specs=vmem,
        scratch_shapes=[
            pltpu.VMEM((2, n, 27, ci, ci), jnp.bfloat16),
            pltpu.VMEM((3, 3, 2, PAD, ci), jnp.bfloat16),
            pltpu.VMEM((2, rows, ci), jnp.bfloat16),
            pltpu.VMEM((2, T, 1, 128), jnp.float32),
            pltpu.VMEM((2, n - 1, rows, ci), jnp.bfloat16),
            pltpu.VMEM((2, n - 1, rows, ci), jnp.bfloat16),
            pltpu.VMEM((rows, ci), jnp.bfloat16),
            dma((2, n, 3)),
            dma((2,)),
            dma((2,)),
            dma((2, T)),
            dma((2, T)),
            dma((2, n - 1)),
            dma((2, n - 1)),
        ],
        compiler_params=pltpu.CompilerParams(
            collective_id=0, has_side_effects=True, vmem_limit_bytes=56 * 2**20
        ),
        cost_estimate=pl.CostEstimate(
            flops=4 * 27 * ci * C * rows, bytes_accessed=4 * 27 * ci * C, transcendentals=0
        ),
    )(lengths, xt, par, w1, w2)
    return out.reshape(frames, cells, ci).transpose(2, 0, 1)


def solution(mesh):
    n, T = mesh.shape["chan"], mesh.shape["tm"]
    c = P("chan")
    cube = P("chan", None, None)
    data = P("chan", "tm", None)
    return jax.shard_map(
        functools.partial(on_device, n, T),
        mesh=mesh,
        in_specs=(data, P(), c, c, cube, c, c, c, cube, c),
        out_specs=data,
        check_vma=False,
    )
```

```python
import functools

import jax
import jax.numpy as jnp
from jax import lax
from jax.experimental import pallas as pl
from jax.experimental.pallas import tpu as pltpu
from jax.sharding import PartitionSpec as P

C = 512
GROUPS = 32
SIZE = C // GROUPS
H = 16
W = 16
CELLS = H * W
PAD = CELLS + 2 * W
EPS = 1e-06
MESH = pl.DeviceIdType.MESH


def iota(shape, dim):
    return lax.broadcasted_iota(jnp.int32, shape, dim)


def dot(a, b):
    return lax.dot_general(a, b, (((1,), (0,)), ((), ())), preferred_element_type=jnp.float32)


def kernel(
    n, T, nclip, wide,
    len_ref, x_ref, g1_ref, b1_ref, c1_ref, g2_ref, b2_ref, c2_ref, w1_ref, w2_ref, out_ref,
    wbuf, hs, halo, stats, lines, psend, precv, ybuf, par,
    w_sem, in_sem, hsend, hrecv, ssend, srecv, qsend, qrecv,
):
    ci = x_ref.shape[2]
    me = lax.axis_index("tm")
    ch = lax.axis_index("chan")

    def peer(d):
        return lax.rem(me + d, T), ch

    def partner(k):
        return me, lax.rem(ch + k, n)

    def w_copy(w_ref, layer, k):
        tgt = lax.rem(ch + k, n)
        if wide:
            src = w_ref.at[:, :, pl.ds(pl.multiple_of(tgt * ci, ci), ci)]
        else:
            src = w_ref.at[tgt]
        return pltpu.make_async_copy(src, wbuf.at[layer, k], w_sem.at[layer, k])

    loads = [pltpu.make_async_copy(x_ref, ybuf.at[0], in_sem.at[6])] + [
        pltpu.make_async_copy(ref, par.at[i], in_sem.at[i])
        for i, ref in enumerate((g1_ref, b1_ref, c1_ref, g2_ref, b2_ref, c2_ref))
    ]
    for load in loads:
        load.start()

    barrier = pltpu.get_barrier_semaphore()

    def greet(d, carry):
        pl.semaphore_signal(barrier, inc=1, device_id=peer(d), device_id_type=MESH)
        return carry

    lax.fori_loop(1, T, greet, 0)
    for k in range(1, n):
        pl.semaphore_signal(barrier, inc=1, device_id=partner(k), device_id_type=MESH)

    for layer, w_ref in enumerate((w1_ref, w2_ref)):
        for k in list(range(1, n)) + [0]:
            w_copy(w_ref, layer, k).start()

    hs[:, :, 0:W, :] = jnp.zeros((3, 2, W, 3 * ci), jnp.bfloat16)
    hs[:, :, W + CELLS :, :] = jnp.zeros((3, 2, W, 3 * ci), jnp.bfloat16)

    @pl.when(me == 0)
    def _():
        halo[...] = jnp.zeros_like(halo)

    first = 2 * me
    starts, counts = [], []
    for f in range(4):
        g = first - 2 + f
        begin = jnp.int32(0)
        count = jnp.int32(0)
        run = jnp.int32(0)
        for c in range(nclip):
            size = len_ref[c]
            inside = jnp.logical_and(run <= g, g < run + size)
            begin = jnp.where(inside, run, begin)
            count = jnp.where(inside, size, count)
            run = run + size
        starts.append(begin)
        counts.append(count)

    def halo_copy(layer, j):
        return pltpu.make_async_remote_copy(
            src_ref=ybuf.at[layer, j], dst_ref=halo.at[layer, j],
            send_sem=hsend.at[layer, j], recv_sem=hrecv.at[layer, j],
            device_id=peer(1), device_id_type=MESH,
        )

    def part_copy(layer, k, j):
        return pltpu.make_async_remote_copy(
            src_ref=psend.at[layer, k, j], dst_ref=precv.at[layer, k, j],
            send_sem=qsend.at[layer, k, j], recv_sem=qrecv.at[layer, k, j],
            device_id=partner(k), device_id_type=MESH,
        )

    def stat_wait(layer, sem):
        every = stats.at[layer, pl.ds(1, T - 1)]
        pltpu.make_async_copy(every, every, sem.at[layer]).wait()

    lane_t = iota((128, ci), 0)
    member = lane_t % 32 == iota((128, ci), 1) // SIZE
    pick_sum = jnp.logical_and(member, lane_t < 64).astype(jnp.bfloat16)
    pick_sq = jnp.logical_and(member, lane_t >= 64).astype(jnp.bfloat16)
    lane_group = (iota((ci, 128), 1) % 32 == iota((ci, 128), 0) // SIZE).astype(jnp.bfloat16)

    def split(a):
        high = a.astype(jnp.bfloat16).astype(jnp.float32)
        rest = a - high
        middle = rest.astype(jnp.bfloat16).astype(jnp.float32)
        low = rest - middle
        return jnp.concatenate([high, middle, low, jnp.zeros_like(a)], axis=0).astype(jnp.bfloat16)

    def gather(parts, zero_one):
        r = dot(parts, zero_one)
        return (r[0:8] + r[8:16]) + r[16:24]

    def frame_sums(j, v):
        lines[j] = jnp.sum(v, axis=0, keepdims=True)
        lines[2 + j] = jnp.sum(v * v, axis=0, keepdims=True)

    def own_stats(layer):
        stacked = jnp.concatenate(
            [lines[q] for q in range(4)] + [jnp.zeros((4, ci), jnp.float32)], axis=0
        )
        by_group = gather(split(stacked), lane_group)
        own = iota((8, 128), 0) == iota((8, 128), 1) // 32
        stats[layer, 0] = jnp.sum(jnp.where(own, by_group, 0.0), axis=0, keepdims=True)

    def send_stats(layer):
        def go(d, carry):
            pltpu.make_async_remote_copy(
                src_ref=stats.at[layer, 0], dst_ref=stats.at[layer, d],
                send_sem=ssend.at[layer], recv_sem=srecv.at[layer],
                device_id=peer(d), device_id_type=MESH,
            ).start()
            return carry

        lax.fori_loop(1, T, go, 0, unroll=True)

    slot = iota((T, 1, 128), 0)
    frame = 2 * jnp.where(slot <= me, me - slot, me - slot + T) + (iota((T, 1, 128), 2) // 32) % 2

    def clip_stats(layer):
        stat_wait(layer, srecv)
        every = stats[layer]
        rows = []
        for f in range(4):
            inside = jnp.logical_and(frame >= starts[f], frame < starts[f] + counts[f])
            total = jnp.sum(jnp.where(inside, every, 0.0), axis=0)
            cells = jnp.maximum(counts[f], 1).astype(jnp.float32) * float(SIZE * CELLS)
            rows.append(total / jnp.full((1, 128), cells))
        parts = split(jnp.concatenate(rows + [jnp.zeros((4, 128), jnp.float32)], axis=0))
        mean = gather(parts, pick_sum)
        var = gather(parts, pick_sq) - mean * mean
        return mean, lax.rsqrt(var + EPS)

    column = iota((CELLS, ci), 0) % W

    def place(f, data, mean, scale, gamma, beta, slots):
        u = (data - mean[f : f + 1]) * (scale[f : f + 1] * gamma) + beta
        h = 0.5 * u * (1.0 + jnp.tanh(0.5 * u))
        before = jnp.where(column == 0, 0.0, pltpu.roll(h, 1, 0))
        after = jnp.where(column == W - 1, 0.0, pltpu.roll(h, CELLS - 1, 0))
        for kw, v in enumerate((before, h, after)):
            for kt, j in slots:
                if kt == 2:
                    kept = v
                else:
                    keep = jnp.full((CELLS, ci), starts[2 + j]) <= first + (j - 2 + kt)
                    kept = jnp.where(keep, v, 0.0)
                hs[kt, j, W : W + CELLS, kw * ci : (kw + 1) * ci] = kept.astype(jnp.bfloat16)

    def run_layer(layer, carry):
        mean, scale = clip_stats(layer)
        gamma, beta, bias = [par[3 * layer + q] for q in range(3)]
        for f, slots in ((2, [(2, 0), (1, 1)]), (3, [(2, 1)])):
            data = ybuf[layer, f - 2].astype(jnp.float32)
            place(f, data, mean, scale, gamma, beta, slots)
        for f, slots in ((0, [(0, 0)]), (1, [(1, 0), (0, 1)])):

            @pl.when(me > 0)
            def _():
                halo_copy(layer, f).wait_recv()

            data = halo[layer, f].astype(jnp.float32)
            place(f, data, mean, scale, gamma, beta, slots)

        def step(i, carry):
            k = lax.rem(i // 2 + 1, n)
            j = lax.rem(i, 2)

            @pl.when(j == 0)
            def _():
                w_copy(w1_ref, layer, k).wait()

            total = None
            for kt in range(3):
                pieces = [hs[kt, j, kh * W : kh * W + CELLS, :] for kh in range(3)]
                if ci % 128 == 0:
                    weights = wbuf[layer, k, 9 * kt : 9 * kt + 9].reshape(9 * ci, ci)
                    terms = [dot(jnp.concatenate(pieces, axis=1), weights)]
                else:
                    terms = [
                        dot(piece, wbuf[layer, k, 9 * kt + 3 * kh : 9 * kt + 3 * kh + 3].reshape(3 * ci, ci))
                        for kh, piece in enumerate(pieces)
                    ]
                for term in terms:
                    total = term if total is None else total + term

            @pl.when(k > 0)
            def _():
                psend[layer, k, j] = total.astype(jnp.bfloat16)
                part_copy(layer, k, j).start()

            @pl.when(k == 0)
            def _():
                out_ref[j] = total + bias

            return carry

        lax.fori_loop(0, 2 * n, step, 0)
        for j in range(2):
            z = out_ref[j]
            for k in range(1, n):
                part_copy(layer, k, j).wait_recv()
                z = z + precv[layer, k, j].astype(jnp.float32)
            y = z.astype(jnp.bfloat16)
            ybuf[layer + 1, j] = y
            out_ref[j] = z

            @pl.when(jnp.logical_and(layer == 0, me < T - 1))
            def _():
                halo_copy(1, j).start()

            frame_sums(j, y.astype(jnp.float32))

        @pl.when(layer == 0)
        def _():
            own_stats(1)
            send_stats(1)

        return carry

    for load in loads:
        load.wait()
    for j in range(2):
        frame_sums(j, ybuf[0, j].astype(jnp.float32))
    own_stats(0)
    pl.semaphore_wait(barrier, T - 1 + n - 1)
    send_stats(0)

    @pl.when(me < T - 1)
    def _():
        for j in range(2):
            halo_copy(0, j).start()

    lax.fori_loop(0, 2, run_layer, 0)
    out_ref[...] += ybuf[0].astype(jnp.float32)

    for layer in range(2):

        @pl.when(me < T - 1)
        def _():
            for j in range(2):
                halo_copy(layer, j).wait_send()

        stat_wait(layer, ssend)
        for k in range(1, n):
            for j in range(2):
                part_copy(layer, k, j).wait_send()


def on_device(n, T, x, lengths, g1, b1, w1, c1, g2, b2, w2, c2):
    ci, frames, cells = x.shape
    wide = ci % 128 == 0
    if wide:
        w1, w2 = [w.transpose(1, 0, 2) for w in (w1, w2)]
    else:
        w1, w2 = [w.reshape(ci, 27, n, ci).transpose(2, 1, 0, 3) for w in (w1, w2)]
    params = [v.reshape(1, ci) for v in (g1, b1, c1, g2, b2, c2)]
    hbm = pl.BlockSpec(memory_space=pl.ANY)
    dma = pltpu.SemaphoreType.DMA
    cube = (2, CELLS, ci)
    out = pl.pallas_call(
        functools.partial(kernel, n, T, lengths.shape[0], wide),
        out_shape=jax.ShapeDtypeStruct(cube, jnp.float32),
        in_specs=[pl.BlockSpec(memory_space=pltpu.SMEM)] + [hbm] * 9,
        out_specs=pl.BlockSpec(memory_space=pltpu.VMEM),
        scratch_shapes=[
            pltpu.VMEM((2, n, 27, ci, ci), jnp.bfloat16),
            pltpu.VMEM((3, 2, PAD, 3 * ci), jnp.bfloat16),
            pltpu.VMEM((2,) + cube, jnp.bfloat16),
            pltpu.VMEM((2, T, 1, 128), jnp.float32),
            pltpu.VMEM((4, 1, ci), jnp.float32),
            pltpu.VMEM((2, n) + cube, jnp.bfloat16),
            pltpu.VMEM((2, n) + cube, jnp.bfloat16),
            pltpu.VMEM((3,) + cube, jnp.bfloat16),
            pltpu.VMEM((6, 1, ci), jnp.float32),
            dma((2, n)),
            dma((7,)),
            dma((2, 2)),
            dma((2, 2)),
            dma((2,)),
            dma((2,)),
            dma((2, n, 2)),
            dma((2, n, 2)),
        ],
        compiler_params=pltpu.CompilerParams(
            collective_id=0, has_side_effects=True, vmem_limit_bytes=56 * 2**20
        ),
        cost_estimate=pl.CostEstimate(
            flops=4 * 27 * ci * C * 2 * CELLS, bytes_accessed=4 * 27 * ci * C, transcendentals=0
        ),
    )(lengths, x.transpose(1, 2, 0), *params, w1, w2)
    return out.transpose(2, 0, 1)


def solution(mesh):
    n, T = mesh.shape["chan"], mesh.shape["tm"]
    c = P("chan")
    cube = P("chan", None, None)
    data = P("chan", "tm", None)
    return jax.shard_map(
        functools.partial(on_device, n, T),
        mesh=mesh,
        in_specs=(data, P(), c, c, cube, c, c, c, cube, c),
        out_specs=data,
        check_vma=False,
    )
```

```python
import functools

import jax
import jax.numpy as jnp
from jax import lax
from jax.experimental import pallas as pl
from jax.experimental.pallas import tpu as pltpu
from jax.sharding import PartitionSpec as P

C = 512
GROUPS = 32
SIZE = C // GROUPS
H = 16
W = 16
CELLS = H * W
PAD = CELLS + 2 * W
HALF = CELLS // 2
EPS = 1e-06
MESH = pl.DeviceIdType.MESH


def iota(shape, dim):
    return lax.broadcasted_iota(jnp.int32, shape, dim)


def dot(a, b):
    return lax.dot_general(a, b, (((1,), (0,)), ((), ())), preferred_element_type=jnp.float32)


def kernel(
    n, T, nclip, wide,
    len_ref, x_ref, g1_ref, b1_ref, c1_ref, g2_ref, b2_ref, c2_ref, w1_ref, w2_ref, out_ref,
    wbuf, hs, halo, stats, lines, psend, precv, ybuf, acc, x_half, x_full, par,
    w_sem, in_sem, hsend, hrecv, ssend, srecv, qsend, qrecv,
):
    ci = x_ref.shape[0] // 4
    me = lax.axis_index("tm")
    ch = lax.axis_index("chan")

    def peer(d):
        return lax.rem(me + d, T), ch

    def partner(k):
        return me, lax.rem(ch + k, n)

    def w_copy(w_ref, layer, k):
        tgt = lax.rem(ch + k, n)
        if wide:
            src = w_ref.at[:, :, pl.ds(pl.multiple_of(tgt * ci, ci), ci)]
        else:
            src = w_ref.at[tgt]
        return pltpu.make_async_copy(src, wbuf.at[layer, k], w_sem.at[layer, k])

    loads = [pltpu.make_async_copy(x_ref, x_half, in_sem.at[6])] + [
        pltpu.make_async_copy(ref, par.at[i], in_sem.at[i])
        for i, ref in enumerate((g1_ref, b1_ref, c1_ref, g2_ref, b2_ref, c2_ref))
    ]
    for load in loads:
        load.start()

    barrier = pltpu.get_barrier_semaphore()

    def greet(d, carry):
        pl.semaphore_signal(barrier, inc=1, device_id=peer(d), device_id_type=MESH)
        return carry

    lax.fori_loop(1, T, greet, 0)
    for k in range(1, n):
        pl.semaphore_signal(barrier, inc=1, device_id=partner(k), device_id_type=MESH)

    for layer, w_ref in enumerate((w1_ref, w2_ref)):
        for k in list(range(1, n)) + [0]:
            w_copy(w_ref, layer, k).start()

    hs[:, :, 0:W, :] = jnp.zeros((3, 2, W, 3 * ci), jnp.bfloat16)
    hs[:, :, W + CELLS :, :] = jnp.zeros((3, 2, W, 3 * ci), jnp.bfloat16)

    @pl.when(me == 0)
    def _():
        halo[...] = jnp.zeros_like(halo)

    first = 2 * me
    starts, counts = [], []
    for f in range(4):
        g = first - 2 + f
        begin = jnp.int32(0)
        count = jnp.int32(0)
        run = jnp.int32(0)
        for c in range(nclip):
            size = len_ref[c]
            inside = jnp.logical_and(run <= g, g < run + size)
            begin = jnp.where(inside, run, begin)
            count = jnp.where(inside, size, count)
            run = run + size
        starts.append(begin)
        counts.append(count)

    def halo_copy(layer, j):
        return pltpu.make_async_remote_copy(
            src_ref=ybuf.at[layer, j], dst_ref=halo.at[layer, j],
            send_sem=hsend.at[layer, j], recv_sem=hrecv.at[layer, j],
            device_id=peer(1), device_id_type=MESH,
        )

    def part_copy(layer, k, piece):
        if isinstance(piece, int) and piece == 2:
            at = (layer, k, 1)
        else:
            at = (layer, k, 0, pl.ds(pl.multiple_of(piece * HALF, HALF), HALF))
        return pltpu.make_async_remote_copy(
            src_ref=psend.at[at], dst_ref=precv.at[at],
            send_sem=qsend.at[layer, k, piece], recv_sem=qrecv.at[layer, k, piece],
            device_id=partner(k), device_id_type=MESH,
        )

    def stat_wait(layer, sem):
        every = stats.at[layer, pl.ds(1, T - 1)]
        pltpu.make_async_copy(every, every, sem.at[layer]).wait()

    lane_t = iota((128, ci), 0)
    member = lane_t % 32 == iota((128, ci), 1) // SIZE
    pick_sum = jnp.logical_and(member, lane_t < 64).astype(jnp.bfloat16)
    pick_sq = jnp.logical_and(member, lane_t >= 64).astype(jnp.bfloat16)
    lane_group = (iota((ci, 128), 1) % 32 == iota((ci, 128), 0) // SIZE).astype(jnp.bfloat16)

    def split(a):
        high = a.astype(jnp.bfloat16).astype(jnp.float32)
        rest = a - high
        middle = rest.astype(jnp.bfloat16).astype(jnp.float32)
        low = rest - middle
        return jnp.concatenate([high, middle, low, jnp.zeros_like(a)], axis=0).astype(jnp.bfloat16)

    def gather(parts, zero_one):
        r = dot(parts, zero_one)
        return (r[0:8] + r[8:16]) + r[16:24]

    def frame_sums(j, v):
        lines[j] = jnp.sum(v, axis=0, keepdims=True)
        lines[2 + j] = jnp.sum(v * v, axis=0, keepdims=True)

    def own_stats(layer):
        stacked = jnp.concatenate(
            [lines[q] for q in range(4)] + [jnp.zeros((4, ci), jnp.float32)], axis=0
        )
        by_group = gather(split(stacked), lane_group)
        own = iota((8, 128), 0) == iota((8, 128), 1) // 32
        stats[layer, 0] = jnp.sum(jnp.where(own, by_group, 0.0), axis=0, keepdims=True)

    def send_stats(layer):
        def go(d, carry):
            pltpu.make_async_remote_copy(
                src_ref=stats.at[layer, 0], dst_ref=stats.at[layer, d],
                send_sem=ssend.at[layer], recv_sem=srecv.at[layer],
                device_id=peer(d), device_id_type=MESH,
            ).start()
            return carry

        lax.fori_loop(1, T, go, 0, unroll=True)

    slot = iota((T, 1, 128), 0)
    frame = 2 * jnp.where(slot <= me, me - slot, me - slot + T) + (iota((T, 1, 128), 2) // 32) % 2

    def clip_stats(layer):
        stat_wait(layer, srecv)
        every = stats[layer]
        rows = []
        for f in range(4):
            inside = jnp.logical_and(frame >= starts[f], frame < starts[f] + counts[f])
            total = jnp.sum(jnp.where(inside, every, 0.0), axis=0)
            cells = jnp.maximum(counts[f], 1).astype(jnp.float32) * float(SIZE * CELLS)
            rows.append(total / jnp.full((1, 128), cells))
        parts = split(jnp.concatenate(rows + [jnp.zeros((4, 128), jnp.float32)], axis=0))
        mean = gather(parts, pick_sum)
        var = gather(parts, pick_sq) - mean * mean
        return mean, lax.rsqrt(var + EPS)

    column = iota((CELLS, ci), 0) % W

    def place(f, data, mean, scale, gamma, beta, slots):
        u = (data - mean[f : f + 1]) * (scale[f : f + 1] * gamma) + beta
        h = 0.5 * u * (1.0 + jnp.tanh(0.5 * u))
        before = jnp.where(column == 0, 0.0, pltpu.roll(h, 1, 0))
        after = jnp.where(column == W - 1, 0.0, pltpu.roll(h, CELLS - 1, 0))
        for kw, v in enumerate((before, h, after)):
            for kt, j in slots:
                if kt == 2:
                    kept = v
                else:
                    keep = jnp.full((CELLS, ci), starts[2 + j]) <= first + (j - 2 + kt)
                    kept = jnp.where(keep, v, 0.0)
                hs[kt, j, W : W + CELLS, kw * ci : (kw + 1) * ci] = kept.astype(jnp.bfloat16)

    def run_layer(layer, carry):
        mean, scale = clip_stats(layer)
        gamma, beta, bias = [par[3 * layer + q] for q in range(3)]
        for f, slots in ((2, [(2, 0), (1, 1)]), (3, [(2, 1)])):
            data = ybuf[layer, f - 2].astype(jnp.float32)
            place(f, data, mean, scale, gamma, beta, slots)
        for f, slots in ((0, [(0, 0)]), (1, [(1, 0), (0, 1)])):

            @pl.when(me > 0)
            def _():
                halo_copy(layer, f).wait_recv()

            data = halo[layer, f].astype(jnp.float32)
            place(f, data, mean, scale, gamma, beta, slots)

        def block(k, j, row, count):
            total = None
            for kt in range(3):
                pieces = [
                    hs[kt, j, pl.ds(pl.multiple_of(row + kh * W, W), count), :] for kh in range(3)
                ]
                if ci % 128 == 0:
                    weights = wbuf[layer, k, 9 * kt : 9 * kt + 9].reshape(9 * ci, ci)
                    terms = [dot(jnp.concatenate(pieces, axis=1), weights)]
                else:
                    terms = [
                        dot(piece, wbuf[layer, k, 9 * kt + 3 * kh : 9 * kt + 3 * kh + 3].reshape(3 * ci, ci))
                        for kh, piece in enumerate(pieces)
                    ]
                for term in terms:
                    total = term if total is None else total + term
            return total

        def early(i, carry):
            k = i // 2 + 1
            half = lax.rem(i, 2)

            @pl.when(half == 0)
            def _():
                w_copy(w1_ref, layer, k).wait()

            row = pl.multiple_of(half * HALF, HALF)
            psend[layer, k, 0, pl.ds(row, HALF), :] = block(k, 0, row, HALF).astype(jnp.bfloat16)
            part_copy(layer, k, half).start()
            return carry

        lax.fori_loop(0, 2 * (n - 1), early, 0)

        def late(i, carry):
            k = jnp.where(i < n, lax.rem(i + 1, n), 0)
            j = jnp.where(i < n, 1, 0)

            @pl.when(i == n - 1)
            def _():
                w_copy(w1_ref, layer, 0).wait()

            total = block(k, j, 0, CELLS)

            @pl.when(i < n - 1)
            def _():
                psend[layer, k, 1] = total.astype(jnp.bfloat16)
                part_copy(layer, k, 2).start()

            @pl.when(i >= n - 1)
            def _():
                acc[j] = total + bias

            return carry

        lax.fori_loop(0, n + 1, late, 0)
        for j in range(2):
            z = acc[j]
            for k in range(1, n):
                for piece in ((0, 1), (2,))[j]:
                    part_copy(layer, k, piece).wait_recv()
                z = z + precv[layer, k, j].astype(jnp.float32)
            y = z.astype(jnp.bfloat16)

            @pl.when(layer == 0)
            def _():
                ybuf[1, j] = y

            @pl.when(layer == 1)
            def _():
                turned = (z + ybuf[0, j].astype(jnp.float32)).T
                for q in range(2):
                    out_ref[pl.ds(2 * q + j, ci, stride=4), :] = turned[:, q * 128 : q * 128 + 128]

            @pl.when(jnp.logical_and(layer == 0, me < T - 1))
            def _():
                halo_copy(1, j).start()

            frame_sums(j, y.astype(jnp.float32))

        @pl.when(layer == 0)
        def _():
            own_stats(1)
            send_stats(1)

        return carry

    for load in loads:
        load.wait()
    x_full[...] = x_half[...].astype(jnp.float32)
    for j in range(2):
        for q in range(2):
            turned = x_full[pl.ds(2 * q + j, ci, stride=4), :].T
            ybuf[0, j, q * 128 : q * 128 + 128, :] = turned.astype(jnp.bfloat16)
        frame_sums(j, ybuf[0, j].astype(jnp.float32))
    own_stats(0)
    pl.semaphore_wait(barrier, T - 1 + n - 1)
    send_stats(0)

    @pl.when(me < T - 1)
    def _():
        for j in range(2):
            halo_copy(0, j).start()

    lax.fori_loop(0, 2, run_layer, 0)

    for layer in range(2):

        @pl.when(me < T - 1)
        def _():
            for j in range(2):
                halo_copy(layer, j).wait_send()

        stat_wait(layer, ssend)
        for k in range(1, n):
            for piece in range(3):
                part_copy(layer, k, piece).wait_send()


def lines_of(x):
    ci, frames, cells = x.shape
    return x.reshape(ci, frames, 2, 128).transpose(0, 2, 1, 3).reshape(4 * ci, 128)


def on_device(n, T, x, lengths, g1, b1, w1, c1, g2, b2, w2, c2):
    ci, frames, cells = x.shape
    wide = ci % 128 == 0
    if wide:
        w1, w2 = [w.transpose(1, 0, 2) for w in (w1, w2)]
    else:
        w1, w2 = [w.reshape(ci, 27, n, ci).transpose(2, 1, 0, 3) for w in (w1, w2)]
    params = [v.reshape(1, ci) for v in (g1, b1, c1, g2, b2, c2)]
    hbm = pl.BlockSpec(memory_space=pl.ANY)
    dma = pltpu.SemaphoreType.DMA
    cube = (2, CELLS, ci)
    out = pl.pallas_call(
        functools.partial(kernel, n, T, lengths.shape[0], wide),
        out_shape=jax.ShapeDtypeStruct((4 * ci, 128), jnp.float32),
        in_specs=[pl.BlockSpec(memory_space=pltpu.SMEM)] + [hbm] * 9,
        out_specs=pl.BlockSpec(memory_space=pltpu.VMEM),
        scratch_shapes=[
            pltpu.VMEM((2, n, 27, ci, ci), jnp.bfloat16),
            pltpu.VMEM((3, 2, PAD, 3 * ci), jnp.bfloat16),
            pltpu.VMEM((2,) + cube, jnp.bfloat16),
            pltpu.VMEM((2, T, 1, 128), jnp.float32),
            pltpu.VMEM((4, 1, ci), jnp.float32),
            pltpu.VMEM((2, n) + cube, jnp.bfloat16),
            pltpu.VMEM((2, n) + cube, jnp.bfloat16),
            pltpu.VMEM((2,) + cube, jnp.bfloat16),
            pltpu.VMEM(cube, jnp.float32),
            pltpu.VMEM((4 * ci, 128), jnp.bfloat16),
            pltpu.VMEM((4 * ci, 128), jnp.float32),
            pltpu.VMEM((6, 1, ci), jnp.float32),
            dma((2, n)),
            dma((7,)),
            dma((2, 2)),
            dma((2, 2)),
            dma((2,)),
            dma((2,)),
            dma((2, n, 3)),
            dma((2, n, 3)),
        ],
        compiler_params=pltpu.CompilerParams(
            collective_id=0, has_side_effects=True, vmem_limit_bytes=56 * 2**20
        ),
        cost_estimate=pl.CostEstimate(
            flops=4 * 27 * ci * C * 2 * CELLS, bytes_accessed=4 * 27 * ci * C, transcendentals=0
        ),
    )(lengths, lines_of(x), *params, w1, w2)
    return out.reshape(ci, 2, frames, 128).transpose(0, 2, 1, 3).reshape(ci, frames, cells)


def solution(mesh):
    n, T = mesh.shape["chan"], mesh.shape["tm"]
    c = P("chan")
    cube = P("chan", None, None)
    data = P("chan", "tm", None)
    return jax.shard_map(
        functools.partial(on_device, n, T),
        mesh=mesh,
        in_specs=(data, P(), c, c, cube, c, c, c, cube, c),
        out_specs=data,
        check_vma=False,
    )
```

```python
import functools

import jax
import jax.numpy as jnp
from jax import lax
from jax.experimental import pallas as pl
from jax.experimental.pallas import tpu as pltpu
from jax.sharding import PartitionSpec as P

C = 512
GROUPS = 32
SIZE = C // GROUPS
H = 16
W = 16
CELLS = H * W
PAD = CELLS + 2 * W
EPS = 1e-06
MESH = pl.DeviceIdType.MESH


def iota(shape, dim):
    return lax.broadcasted_iota(jnp.int32, shape, dim)


def dot(a, b):
    return lax.dot_general(a, b, (((1,), (0,)), ((), ())), preferred_element_type=jnp.float32)


def kernel(
    n, T, nclip, wide,
    len_ref, x_ref, g1_ref, b1_ref, c1_ref, g2_ref, b2_ref, c2_ref, w1_ref, w2_ref, out_ref,
    wbuf, hs, halo, stats, lines, psend, precv, ybuf, acc, x_half, x_full, par,
    w_sem, in_sem, hsend, hrecv, ssend, srecv, qsend, qrecv,
):
    ci = x_ref.shape[0] // 4
    me = lax.axis_index("tm")
    ch = lax.axis_index("chan")

    def peer(d):
        return lax.rem(me + d, T), ch

    def partner(k):
        return me, lax.rem(ch + k, n)

    def w_copy(w_ref, layer, k):
        tgt = lax.rem(ch + k, n)
        if wide:
            src = w_ref.at[:, :, pl.ds(pl.multiple_of(tgt * ci, ci), ci)]
        else:
            src = w_ref.at[tgt]
        return pltpu.make_async_copy(src, wbuf.at[layer, k], w_sem.at[layer, k])

    barrier = pltpu.get_barrier_semaphore()

    def greet(d, carry):
        pl.semaphore_signal(barrier, inc=1, device_id=peer(d), device_id_type=MESH)
        return carry

    lax.fori_loop(1, T, greet, 0)
    for k in range(1, n):
        pl.semaphore_signal(barrier, inc=1, device_id=partner(k), device_id_type=MESH)

    loads = [pltpu.make_async_copy(x_ref, x_half, in_sem.at[6])] + [
        pltpu.make_async_copy(ref, par.at[i], in_sem.at[i])
        for i, ref in enumerate((g1_ref, b1_ref, c1_ref, g2_ref, b2_ref, c2_ref))
    ]
    for load in loads:
        load.start()

    for layer, w_ref in enumerate((w1_ref, w2_ref)):
        for k in list(range(1, n)) + [0]:
            w_copy(w_ref, layer, k).start()

    hs[:, :, 0:W, :] = jnp.zeros((3, 2, W, 3 * ci), jnp.bfloat16)
    hs[:, :, W + CELLS :, :] = jnp.zeros((3, 2, W, 3 * ci), jnp.bfloat16)

    @pl.when(me == 0)
    def _():
        halo[...] = jnp.zeros_like(halo)

    first = 2 * me
    starts, counts = [], []
    for f in range(4):
        g = first - 2 + f
        begin = jnp.int32(0)
        count = jnp.int32(0)
        run = jnp.int32(0)
        for c in range(nclip):
            size = len_ref[c]
            inside = jnp.logical_and(run <= g, g < run + size)
            begin = jnp.where(inside, run, begin)
            count = jnp.where(inside, size, count)
            run = run + size
        starts.append(begin)
        counts.append(count)

    def halo_copy(layer, j):
        return pltpu.make_async_remote_copy(
            src_ref=ybuf.at[layer, j], dst_ref=halo.at[layer, j],
            send_sem=hsend.at[layer, j], recv_sem=hrecv.at[layer, j],
            device_id=peer(1), device_id_type=MESH,
        )

    def part_copy(layer, k, j):
        return pltpu.make_async_remote_copy(
            src_ref=psend.at[layer, k, j], dst_ref=precv.at[layer, k, j],
            send_sem=qsend.at[layer, k, j], recv_sem=qrecv.at[layer, k, j],
            device_id=partner(k), device_id_type=MESH,
        )

    def stat_wait(layer, sem):
        every = stats.at[layer, pl.ds(1, T - 1)]
        pltpu.make_async_copy(every, every, sem.at[layer]).wait()

    lane_t = iota((128, ci), 0)
    member = lane_t % 32 == iota((128, ci), 1) // SIZE
    pick_sum = jnp.logical_and(member, lane_t < 64).astype(jnp.bfloat16)
    pick_sq = jnp.logical_and(member, lane_t >= 64).astype(jnp.bfloat16)
    lane_group = (iota((ci, 128), 1) % 32 == iota((ci, 128), 0) // SIZE).astype(jnp.bfloat16)

    def split(a):
        high = a.astype(jnp.bfloat16).astype(jnp.float32)
        rest = a - high
        middle = rest.astype(jnp.bfloat16).astype(jnp.float32)
        low = rest - middle
        return jnp.concatenate([high, middle, low, jnp.zeros_like(a)], axis=0).astype(jnp.bfloat16)

    def gather(parts, zero_one):
        r = dot(parts, zero_one)
        return (r[0:8] + r[8:16]) + r[16:24]

    def frame_sums(j, v):
        lines[j] = jnp.sum(v, axis=0, keepdims=True)
        lines[2 + j] = jnp.sum(v * v, axis=0, keepdims=True)

    def own_stats(layer):
        stacked = jnp.concatenate(
            [lines[q] for q in range(4)] + [jnp.zeros((4, ci), jnp.float32)], axis=0
        )
        by_group = gather(split(stacked), lane_group)
        own = iota((8, 128), 0) == iota((8, 128), 1) // 32
        stats[layer, 0] = jnp.sum(jnp.where(own, by_group, 0.0), axis=0, keepdims=True)

    def send_stats(layer):
        def go(d, carry):
            pltpu.make_async_remote_copy(
                src_ref=stats.at[layer, 0], dst_ref=stats.at[layer, d],
                send_sem=ssend.at[layer], recv_sem=srecv.at[layer],
                device_id=peer(d), device_id_type=MESH,
            ).start()
            return carry

        lax.fori_loop(1, T, go, 0, unroll=True)

    slot = iota((T, 1, 128), 0)
    frame = 2 * jnp.where(slot <= me, me - slot, me - slot + T) + (iota((T, 1, 128), 2) // 32) % 2

    def clip_stats(layer):
        stat_wait(layer, srecv)
        every = stats[layer]
        rows = []
        for f in range(4):
            inside = jnp.logical_and(frame >= starts[f], frame < starts[f] + counts[f])
            total = jnp.sum(jnp.where(inside, every, 0.0), axis=0)
            cells = jnp.maximum(counts[f], 1).astype(jnp.float32) * float(SIZE * CELLS)
            rows.append(total / jnp.full((1, 128), cells))
        parts = split(jnp.concatenate(rows + [jnp.zeros((4, 128), jnp.float32)], axis=0))
        mean = gather(parts, pick_sum)
        var = gather(parts, pick_sq) - mean * mean
        return mean, lax.rsqrt(var + EPS)

    column = iota((CELLS, ci), 0) % W

    def place(f, data, mean, scale, gamma, beta, slots):
        u = (data - mean[f : f + 1]) * (scale[f : f + 1] * gamma) + beta
        h = 0.5 * u * (1.0 + jnp.tanh(0.5 * u))
        before = jnp.where(column == 0, 0.0, pltpu.roll(h, 1, 0))
        after = jnp.where(column == W - 1, 0.0, pltpu.roll(h, CELLS - 1, 0))
        for kw, v in enumerate((before, h, after)):
            for kt, j in slots:
                if kt == 2:
                    kept = v
                else:
                    keep = jnp.full((CELLS, ci), starts[2 + j]) <= first + (j - 2 + kt)
                    kept = jnp.where(keep, v, 0.0)
                hs[kt, j, W : W + CELLS, kw * ci : (kw + 1) * ci] = kept.astype(jnp.bfloat16)

    def run_layer(layer, carry):
        mean, scale = clip_stats(layer)
        gamma, beta, bias = [par[3 * layer + q] for q in range(3)]
        data = ybuf[layer, 0].astype(jnp.float32)
        place(2, data, mean, scale, gamma, beta, [(2, 0), (1, 1)])
        for f, slots in ((0, [(0, 0)]), (1, [(1, 0), (0, 1)])):

            @pl.when(me > 0)
            def _():
                halo_copy(layer, f).wait_recv()

            data = halo[layer, f].astype(jnp.float32)
            place(f, data, mean, scale, gamma, beta, slots)

        def block(k, frames):
            total = None
            for kt in range(3):
                pieces = [
                    hs[kt, frames, kh * W : kh * W + CELLS, :].reshape(-1, 3 * ci)
                    for kh in range(3)
                ]
                if ci % 128 == 0:
                    weights = wbuf[layer, k, 9 * kt : 9 * kt + 9].reshape(9 * ci, ci)
                    terms = [dot(jnp.concatenate(pieces, axis=1), weights)]
                else:
                    terms = [
                        dot(piece, wbuf[layer, k, 9 * kt + 3 * kh : 9 * kt + 3 * kh + 3].reshape(3 * ci, ci))
                        for kh, piece in enumerate(pieces)
                    ]
                for term in terms:
                    total = term if total is None else total + term
            return total

        def for_partner(i, carry):
            k = i // 2 + 1
            j = lax.rem(i, 2)

            @pl.when(j == 0)
            def _():
                w_copy(w1_ref, layer, k).wait()

            @pl.when(i == 1)
            def _():
                data = ybuf[layer, 1].astype(jnp.float32)
                place(3, data, mean, scale, gamma, beta, [(2, 1)])

            psend[layer, k, j] = block(k, j).astype(jnp.bfloat16)
            part_copy(layer, k, j).start()
            return carry

        lax.fori_loop(0, 2 * (n - 1), for_partner, 0)
        w_copy(w1_ref, layer, 0).wait()
        acc[...] = (block(0, slice(0, 2)) + bias).reshape(2, CELLS, ci)
        for j in range(2):
            z = acc[j]
            for k in range(1, n):
                part_copy(layer, k, j).wait_recv()
                z = z + precv[layer, k, j].astype(jnp.float32)
            y = z.astype(jnp.bfloat16)

            @pl.when(layer == 0)
            def _():
                ybuf[1, j] = y

            @pl.when(layer == 1)
            def _():
                turned = (z + ybuf[0, j].astype(jnp.float32)).T
                for q in range(2):
                    out_ref[pl.ds(2 * q + j, ci, stride=4), :] = turned[:, q * 128 : q * 128 + 128]

            @pl.when(jnp.logical_and(layer == 0, me < T - 1))
            def _():
                halo_copy(1, j).start()

            frame_sums(j, y.astype(jnp.float32))

        @pl.when(layer == 0)
        def _():
            own_stats(1)
            send_stats(1)

        return carry

    for load in loads:
        load.wait()
    x_full[...] = x_half[...].astype(jnp.float32)
    for j in range(2):
        for q in range(2):
            turned = x_full[pl.ds(2 * q + j, ci, stride=4), :].T
            ybuf[0, j, q * 128 : q * 128 + 128, :] = turned.astype(jnp.bfloat16)
        frame_sums(j, ybuf[0, j].astype(jnp.float32))
    own_stats(0)
    pl.semaphore_wait(barrier, T - 1 + n - 1)
    send_stats(0)

    @pl.when(me < T - 1)
    def _():
        for j in range(2):
            halo_copy(0, j).start()

    lax.fori_loop(0, 2, run_layer, 0)

    for layer in range(2):

        @pl.when(me < T - 1)
        def _():
            for j in range(2):
                halo_copy(layer, j).wait_send()

        stat_wait(layer, ssend)
        for k in range(1, n):
            for j in range(2):
                part_copy(layer, k, j).wait_send()


def lines_of(x):
    ci, frames, cells = x.shape
    return x.reshape(ci, frames, 2, 128).transpose(0, 2, 1, 3).reshape(4 * ci, 128)


def on_device(n, T, x, lengths, g1, b1, w1, c1, g2, b2, w2, c2):
    ci, frames, cells = x.shape
    wide = ci % 128 == 0
    if wide:
        w1, w2 = [w.transpose(1, 0, 2) for w in (w1, w2)]
    else:
        w1, w2 = [w.reshape(ci, 27, n, ci).transpose(2, 1, 0, 3) for w in (w1, w2)]
    params = [v.reshape(1, ci) for v in (g1, b1, c1, g2, b2, c2)]
    hbm = pl.BlockSpec(memory_space=pl.ANY)
    dma = pltpu.SemaphoreType.DMA
    cube = (2, CELLS, ci)
    out = pl.pallas_call(
        functools.partial(kernel, n, T, lengths.shape[0], wide),
        out_shape=jax.ShapeDtypeStruct((4 * ci, 128), jnp.float32),
        in_specs=[pl.BlockSpec(memory_space=pltpu.SMEM)] + [hbm] * 9,
        out_specs=pl.BlockSpec(memory_space=pltpu.VMEM),
        scratch_shapes=[
            pltpu.VMEM((2, n, 27, ci, ci), jnp.bfloat16),
            pltpu.VMEM((3, 2, PAD, 3 * ci), jnp.bfloat16),
            pltpu.VMEM((2,) + cube, jnp.bfloat16),
            pltpu.VMEM((2, T, 1, 128), jnp.float32),
            pltpu.VMEM((4, 1, ci), jnp.float32),
            pltpu.VMEM((2, n) + cube, jnp.bfloat16),
            pltpu.VMEM((2, n) + cube, jnp.bfloat16),
            pltpu.VMEM((2,) + cube, jnp.bfloat16),
            pltpu.VMEM(cube, jnp.float32),
            pltpu.VMEM((4 * ci, 128), jnp.bfloat16),
            pltpu.VMEM((4 * ci, 128), jnp.float32),
            pltpu.VMEM((6, 1, ci), jnp.float32),
            dma((2, n)),
            dma((7,)),
            dma((2, 2)),
            dma((2, 2)),
            dma((2,)),
            dma((2,)),
            dma((2, n, 2)),
            dma((2, n, 2)),
        ],
        compiler_params=pltpu.CompilerParams(
            collective_id=0, has_side_effects=True, vmem_limit_bytes=56 * 2**20
        ),
        cost_estimate=pl.CostEstimate(
            flops=4 * 27 * ci * C * 2 * CELLS, bytes_accessed=4 * 27 * ci * C, transcendentals=0
        ),
    )(lengths, lines_of(x), *params, w1, w2)
    return out.reshape(ci, 2, frames, 128).transpose(0, 2, 1, 3).reshape(ci, frames, cells)


def solution(mesh):
    n, T = mesh.shape["chan"], mesh.shape["tm"]
    c = P("chan")
    cube = P("chan", None, None)
    data = P("chan", "tm", None)
    return jax.shard_map(
        functools.partial(on_device, n, T),
        mesh=mesh,
        in_specs=(data, P(), c, c, cube, c, c, c, cube, c),
        out_specs=data,
        check_vma=False,
    )
```

```python
import functools

import jax
import jax.numpy as jnp
from jax import lax
from jax.experimental import pallas as pl
from jax.experimental.pallas import tpu as pltpu
from jax.sharding import PartitionSpec as P

C = 512
GROUPS = 32
SIZE = C // GROUPS
H = 16
W = 16
CELLS = H * W
PAD = CELLS + 2 * W
HALF = CELLS // 2
EPS = 1e-06
MESH = pl.DeviceIdType.MESH


def iota(shape, dim):
    return lax.broadcasted_iota(jnp.int32, shape, dim)


def dot(a, b):
    return lax.dot_general(a, b, (((1,), (0,)), ((), ())), preferred_element_type=jnp.float32)


def kernel(
    n, T, nclip, wide,
    len_ref, x_ref, g1_ref, b1_ref, c1_ref, g2_ref, b2_ref, c2_ref, w1_ref, w2_ref, out_ref,
    wbuf, hs, halo, stats, lines, psend, precv, ybuf, acc, x_half, x_full, par,
    w_sem, in_sem, hsend, hrecv, ssend, srecv, qsend, qrecv,
):
    ci = x_ref.shape[0] // 4
    me = lax.axis_index("tm")
    ch = lax.axis_index("chan")

    def peer(d):
        return lax.rem(me + d, T), ch

    def partner(k):
        return me, lax.rem(ch + k, n)

    def w_copy(w_ref, layer, k):
        tgt = lax.rem(ch + k, n)
        if wide:
            src = w_ref.at[:, :, pl.ds(pl.multiple_of(tgt * ci, ci), ci)]
        else:
            src = w_ref.at[tgt]
        return pltpu.make_async_copy(src, wbuf.at[layer, k], w_sem.at[layer, k])

    barrier = pltpu.get_barrier_semaphore()

    def greet(d, carry):
        pl.semaphore_signal(barrier, inc=1, device_id=peer(d), device_id_type=MESH)
        return carry

    lax.fori_loop(1, T, greet, 0)
    for k in range(1, n):
        pl.semaphore_signal(barrier, inc=1, device_id=partner(k), device_id_type=MESH)

    loads = [pltpu.make_async_copy(x_ref, x_half, in_sem.at[6])] + [
        pltpu.make_async_copy(ref, par.at[i], in_sem.at[i])
        for i, ref in enumerate((g1_ref, b1_ref, c1_ref, g2_ref, b2_ref, c2_ref))
    ]
    for load in loads:
        load.start()

    for layer, w_ref in enumerate((w1_ref, w2_ref)):
        for k in list(range(1, n)) + [0]:
            w_copy(w_ref, layer, k).start()

    hs[:, :, 0:W, :] = jnp.zeros((3, 2, W, 3 * ci), jnp.bfloat16)
    hs[:, :, W + CELLS :, :] = jnp.zeros((3, 2, W, 3 * ci), jnp.bfloat16)

    @pl.when(me == 0)
    def _():
        halo[...] = jnp.zeros_like(halo)

    first = 2 * me
    starts, counts = [], []
    for f in range(4):
        g = first - 2 + f
        begin = jnp.int32(0)
        count = jnp.int32(0)
        run = jnp.int32(0)
        for c in range(nclip):
            size = len_ref[c]
            inside = jnp.logical_and(run <= g, g < run + size)
            begin = jnp.where(inside, run, begin)
            count = jnp.where(inside, size, count)
            run = run + size
        starts.append(begin)
        counts.append(count)

    def halo_copy(layer, j):
        return pltpu.make_async_remote_copy(
            src_ref=ybuf.at[layer, j], dst_ref=halo.at[layer, j],
            send_sem=hsend.at[layer, j], recv_sem=hrecv.at[layer, j],
            device_id=peer(1), device_id_type=MESH,
        )

    def part_copy(layer, k, piece):
        if isinstance(piece, int) and piece == 2:
            at = (layer, k, 1)
        else:
            at = (layer, k, 0, pl.ds(pl.multiple_of(piece * HALF, HALF), HALF))
        return pltpu.make_async_remote_copy(
            src_ref=psend.at[at], dst_ref=precv.at[at],
            send_sem=qsend.at[layer, k, piece], recv_sem=qrecv.at[layer, k, piece],
            device_id=partner(k), device_id_type=MESH,
        )

    def stat_wait(layer, sem):
        every = stats.at[layer, pl.ds(1, T - 1)]
        pltpu.make_async_copy(every, every, sem.at[layer]).wait()

    lane_t = iota((128, ci), 0)
    member = lane_t % 32 == iota((128, ci), 1) // SIZE
    pick_sum = jnp.logical_and(member, lane_t < 64).astype(jnp.bfloat16)
    pick_sq = jnp.logical_and(member, lane_t >= 64).astype(jnp.bfloat16)
    lane_group = (iota((ci, 128), 1) % 32 == iota((ci, 128), 0) // SIZE).astype(jnp.bfloat16)

    def split(a):
        high = a.astype(jnp.bfloat16).astype(jnp.float32)
        rest = a - high
        middle = rest.astype(jnp.bfloat16).astype(jnp.float32)
        low = rest - middle
        return jnp.concatenate([high, middle, low, jnp.zeros_like(a)], axis=0).astype(jnp.bfloat16)

    def gather(parts, zero_one):
        r = dot(parts, zero_one)
        return (r[0:8] + r[8:16]) + r[16:24]

    def frame_sums(j, v):
        lines[j] = jnp.sum(v, axis=0, keepdims=True)
        lines[2 + j] = jnp.sum(v * v, axis=0, keepdims=True)

    def own_stats(layer):
        stacked = jnp.concatenate(
            [lines[q] for q in range(4)] + [jnp.zeros((4, ci), jnp.float32)], axis=0
        )
        by_group = gather(split(stacked), lane_group)
        own = iota((8, 128), 0) == iota((8, 128), 1) // 32
        stats[layer, 0] = jnp.sum(jnp.where(own, by_group, 0.0), axis=0, keepdims=True)

    def send_stats(layer):
        def go(d, carry):
            pltpu.make_async_remote_copy(
                src_ref=stats.at[layer, 0], dst_ref=stats.at[layer, d],
                send_sem=ssend.at[layer], recv_sem=srecv.at[layer],
                device_id=peer(d), device_id_type=MESH,
            ).start()
            return carry

        lax.fori_loop(1, T, go, 0, unroll=True)

    slot = iota((T, 1, 128), 0)
    frame = 2 * jnp.where(slot <= me, me - slot, me - slot + T) + (iota((T, 1, 128), 2) // 32) % 2

    def clip_stats(layer):
        stat_wait(layer, srecv)
        every = stats[layer]
        rows = []
        for f in range(4):
            inside = jnp.logical_and(frame >= starts[f], frame < starts[f] + counts[f])
            total = jnp.sum(jnp.where(inside, every, 0.0), axis=0)
            cells = jnp.maximum(counts[f], 1).astype(jnp.float32) * float(SIZE * CELLS)
            rows.append(total / jnp.full((1, 128), cells))
        parts = split(jnp.concatenate(rows + [jnp.zeros((4, 128), jnp.float32)], axis=0))
        mean = gather(parts, pick_sum)
        var = gather(parts, pick_sq) - mean * mean
        return mean, lax.rsqrt(var + EPS)

    column = iota((CELLS, ci), 0) % W

    def place(f, data, mean, scale, gamma, beta, slots):
        u = (data - mean[f : f + 1]) * (scale[f : f + 1] * gamma) + beta
        h = 0.5 * u * (1.0 + jnp.tanh(0.5 * u))
        before = jnp.where(column == 0, 0.0, pltpu.roll(h, 1, 0))
        after = jnp.where(column == W - 1, 0.0, pltpu.roll(h, CELLS - 1, 0))
        for kw, v in enumerate((before, h, after)):
            for kt, j in slots:
                if kt == 2:
                    kept = v
                else:
                    keep = jnp.full((CELLS, ci), starts[2 + j]) <= first + (j - 2 + kt)
                    kept = jnp.where(keep, v, 0.0)
                hs[kt, j, W : W + CELLS, kw * ci : (kw + 1) * ci] = kept.astype(jnp.bfloat16)

    def run_layer(layer, carry):
        mean, scale = clip_stats(layer)
        gamma, beta, bias = [par[3 * layer + q] for q in range(3)]
        data = ybuf[layer, 0].astype(jnp.float32)
        place(2, data, mean, scale, gamma, beta, [(2, 0), (1, 1)])
        for f, slots in ((0, [(0, 0)]), (1, [(1, 0), (0, 1)])):

            @pl.when(me > 0)
            def _():
                halo_copy(layer, f).wait_recv()

            data = halo[layer, f].astype(jnp.float32)
            place(f, data, mean, scale, gamma, beta, slots)

        def block(k, j, row, count):
            total = None
            for kt in range(3):
                pieces = [
                    hs[kt, j, pl.ds(pl.multiple_of(row + kh * W, W), count), :] for kh in range(3)
                ]
                if ci % 128 == 0:
                    weights = wbuf[layer, k, 9 * kt : 9 * kt + 9].reshape(9 * ci, ci)
                    terms = [dot(jnp.concatenate(pieces, axis=1), weights)]
                else:
                    terms = [
                        dot(piece, wbuf[layer, k, 9 * kt + 3 * kh : 9 * kt + 3 * kh + 3].reshape(3 * ci, ci))
                        for kh, piece in enumerate(pieces)
                    ]
                for term in terms:
                    total = term if total is None else total + term
            return total

        def early(i, carry):
            k = i // 2 + 1
            half = lax.rem(i, 2)

            @pl.when(half == 0)
            def _():
                w_copy(w1_ref, layer, k).wait()

            row = pl.multiple_of(half * HALF, HALF)
            psend[layer, k, 0, pl.ds(row, HALF), :] = block(k, 0, row, HALF).astype(jnp.bfloat16)
            part_copy(layer, k, half).start()
            return carry

        lax.fori_loop(0, 2 * (n - 1), early, 0)
        data = ybuf[layer, 1].astype(jnp.float32)
        place(3, data, mean, scale, gamma, beta, [(2, 1)])

        def late(i, carry):
            k = jnp.where(i < n, lax.rem(i + 1, n), 0)
            j = jnp.where(i < n, 1, 0)

            @pl.when(i == n - 1)
            def _():
                w_copy(w1_ref, layer, 0).wait()

            total = block(k, j, 0, CELLS)

            @pl.when(i < n - 1)
            def _():
                psend[layer, k, 1] = total.astype(jnp.bfloat16)
                part_copy(layer, k, 2).start()

            @pl.when(i >= n - 1)
            def _():
                acc[j] = total + bias

            return carry

        lax.fori_loop(0, n + 1, late, 0)
        for j in range(2):
            z = acc[j]
            for k in range(1, n):
                for piece in ((0, 1), (2,))[j]:
                    part_copy(layer, k, piece).wait_recv()
                z = z + precv[layer, k, j].astype(jnp.float32)
            y = z.astype(jnp.bfloat16)

            @pl.when(layer == 0)
            def _():
                ybuf[1, j] = y

            @pl.when(layer == 1)
            def _():
                turned = (z + ybuf[0, j].astype(jnp.float32)).T
                for q in range(2):
                    out_ref[pl.ds(2 * q + j, ci, stride=4), :] = turned[:, q * 128 : q * 128 + 128]

            @pl.when(jnp.logical_and(layer == 0, me < T - 1))
            def _():
                halo_copy(1, j).start()

            frame_sums(j, y.astype(jnp.float32))

        @pl.when(layer == 0)
        def _():
            own_stats(1)
            send_stats(1)

        return carry

    for load in loads:
        load.wait()
    x_full[...] = x_half[...].astype(jnp.float32)
    for j in range(2):
        for q in range(2):
            turned = x_full[pl.ds(2 * q + j, ci, stride=4), :].T
            ybuf[0, j, q * 128 : q * 128 + 128, :] = turned.astype(jnp.bfloat16)
        frame_sums(j, ybuf[0, j].astype(jnp.float32))
    own_stats(0)
    pl.semaphore_wait(barrier, T - 1 + n - 1)
    send_stats(0)

    @pl.when(me < T - 1)
    def _():
        for j in range(2):
            halo_copy(0, j).start()

    lax.fori_loop(0, 2, run_layer, 0)

    for layer in range(2):

        @pl.when(me < T - 1)
        def _():
            for j in range(2):
                halo_copy(layer, j).wait_send()

        stat_wait(layer, ssend)
        for k in range(1, n):
            for piece in range(3):
                part_copy(layer, k, piece).wait_send()


def hand_over(from_ref, to_ref, sems):
    size = from_ref.shape[0] // 8
    copies = [
        pltpu.make_async_copy(
            from_ref.at[pl.ds(i * size, size)], to_ref.at[pl.ds(i * size, size)], sems.at[i]
        )
        for i in range(8)
    ]
    for copy in copies:
        copy.start()
    for copy in copies:
        copy.wait()


def lines_of(x):
    ci, frames, cells = x.shape
    return x.reshape(ci, frames, 2, 128).transpose(0, 2, 1, 3).reshape(4 * ci, 128)


def on_device(n, T, x, lengths, g1, b1, w1, c1, g2, b2, w2, c2):
    ci, frames, cells = x.shape
    wide = ci % 128 == 0
    if wide:
        w1, w2 = [w.transpose(1, 0, 2) for w in (w1, w2)]
    else:
        w1, w2 = [w.reshape(ci, 27, n, ci).transpose(2, 1, 0, 3) for w in (w1, w2)]
    params = [v.reshape(1, ci) for v in (g1, b1, c1, g2, b2, c2)]
    hbm = pl.BlockSpec(memory_space=pl.ANY)
    dma = pltpu.SemaphoreType.DMA
    cube = (2, CELLS, ci)
    out = pl.pallas_call(
        functools.partial(kernel, n, T, lengths.shape[0], wide),
        out_shape=jax.ShapeDtypeStruct((4 * ci, 128), jnp.float32),
        in_specs=[pl.BlockSpec(memory_space=pltpu.SMEM)] + [hbm] * 9,
        out_specs=pl.BlockSpec(memory_space=pltpu.VMEM),
        scratch_shapes=[
            pltpu.VMEM((2, n, 27, ci, ci), jnp.bfloat16),
            pltpu.VMEM((3, 2, PAD, 3 * ci), jnp.bfloat16),
            pltpu.VMEM((2,) + cube, jnp.bfloat16),
            pltpu.VMEM((2, T, 1, 128), jnp.float32),
            pltpu.VMEM((4, 1, ci), jnp.float32),
            pltpu.VMEM((2, n) + cube, jnp.bfloat16),
            pltpu.VMEM((2, n) + cube, jnp.bfloat16),
            pltpu.VMEM((2,) + cube, jnp.bfloat16),
            pltpu.VMEM(cube, jnp.float32),
            pltpu.VMEM((4 * ci, 128), jnp.bfloat16),
            pltpu.VMEM((4 * ci, 128), jnp.float32),
            pltpu.VMEM((6, 1, ci), jnp.float32),
            dma((2, n)),
            dma((7,)),
            dma((2, 2)),
            dma((2, 2)),
            dma((2,)),
            dma((2,)),
            dma((2, n, 3)),
            dma((2, n, 3)),
        ],
        compiler_params=pltpu.CompilerParams(
            collective_id=0, has_side_effects=True, vmem_limit_bytes=56 * 2**20
        ),
        cost_estimate=pl.CostEstimate(
            flops=4 * 27 * ci * C * 2 * CELLS, bytes_accessed=4 * 27 * ci * C, transcendentals=0
        ),
    )(lengths, lines_of(x), *params, w1, w2)
    out = pl.pallas_call(
        hand_over,
        out_shape=jax.ShapeDtypeStruct(out.shape, out.dtype),
        in_specs=[hbm],
        out_specs=hbm,
        scratch_shapes=[dma((8,))],
        compiler_params=pltpu.CompilerParams(vmem_limit_bytes=56 * 2**20),
    )(out)
    return out.reshape(ci, 2, frames, 128).transpose(0, 2, 1, 3).reshape(ci, frames, cells)


def solution(mesh):
    n, T = mesh.shape["chan"], mesh.shape["tm"]
    c = P("chan")
    cube = P("chan", None, None)
    data = P("chan", "tm", None)
    return jax.shard_map(
        functools.partial(on_device, n, T),
        mesh=mesh,
        in_specs=(data, P(), c, c, cube, c, c, c, cube, c),
        out_specs=data,
        check_vma=False,
    )
```

```python
import functools

import jax
import jax.numpy as jnp
from jax import lax
from jax.experimental import pallas as pl
from jax.experimental.pallas import tpu as pltpu
from jax.sharding import PartitionSpec as P

C = 512
GROUPS = 32
SIZE = C // GROUPS
H = 16
W = 16
CELLS = H * W
PAD = CELLS + 2 * W
HALF = CELLS // 2
EPS = 1e-06
MESH = pl.DeviceIdType.MESH


def iota(shape, dim):
    return lax.broadcasted_iota(jnp.int32, shape, dim)


def dot(a, b):
    return lax.dot_general(a, b, (((1,), (0,)), ((), ())), preferred_element_type=jnp.float32)


def kernel(
    n, T, nclip, wide,
    len_ref, x_ref, g1_ref, b1_ref, c1_ref, g2_ref, b2_ref, c2_ref, w1_ref, w2_ref, out_ref,
    wbuf, hs, halo, stats, lines, psend, precv, ybuf, acc, x_half, x_full, par,
    w_sem, in_sem, hsend, hrecv, ssend, srecv, qsend, qrecv,
):
    ci = x_ref.shape[0] // 4
    me = lax.axis_index("tm")
    ch = lax.axis_index("chan")

    def peer(d):
        return lax.rem(me + d, T), ch

    def partner(k):
        return me, lax.rem(ch + k, n)

    def w_copy(w_ref, layer, k):
        tgt = lax.rem(ch + k, n)
        if wide:
            src = w_ref.at[:, :, pl.ds(pl.multiple_of(tgt * ci, ci), ci)]
        else:
            src = w_ref.at[tgt]
        return pltpu.make_async_copy(src, wbuf.at[layer, k], w_sem.at[layer, k])

    loads = [pltpu.make_async_copy(x_ref, x_half, in_sem.at[6])] + [
        pltpu.make_async_copy(ref, par.at[i], in_sem.at[i])
        for i, ref in enumerate((g1_ref, b1_ref, c1_ref, g2_ref, b2_ref, c2_ref))
    ]
    for load in loads:
        load.start()

    barrier = pltpu.get_barrier_semaphore()

    def greet(d, carry):
        pl.semaphore_signal(barrier, inc=1, device_id=peer(d), device_id_type=MESH)
        return carry

    lax.fori_loop(1, T, greet, 0)
    for k in range(1, n):
        pl.semaphore_signal(barrier, inc=1, device_id=partner(k), device_id_type=MESH)

    for layer, w_ref in enumerate((w1_ref, w2_ref)):
        for k in list(range(1, n)) + [0]:
            w_copy(w_ref, layer, k).start()

    def halo_copy(layer, j):
        return pltpu.make_async_remote_copy(
            src_ref=ybuf.at[layer, j], dst_ref=halo.at[layer, j],
            send_sem=hsend.at[layer, j], recv_sem=hrecv.at[layer, j],
            device_id=peer(1), device_id_type=MESH,
        )

    def part_copy(layer, k, piece):
        if isinstance(piece, int) and piece == 2:
            at = (layer, k, 1)
        else:
            at = (layer, k, 0, pl.ds(pl.multiple_of(piece * HALF, HALF), HALF))
        return pltpu.make_async_remote_copy(
            src_ref=psend.at[at], dst_ref=precv.at[at],
            send_sem=qsend.at[layer, k, piece], recv_sem=qrecv.at[layer, k, piece],
            device_id=partner(k), device_id_type=MESH,
        )

    def stat_wait(layer, sem):
        every = stats.at[layer, pl.ds(1, T - 1)]
        pltpu.make_async_copy(every, every, sem.at[layer]).wait()

    lane_t = iota((128, ci), 0)
    member = lane_t % 32 == iota((128, ci), 1) // SIZE
    pick_sum = jnp.logical_and(member, lane_t < 64).astype(jnp.bfloat16)
    pick_sq = jnp.logical_and(member, lane_t >= 64).astype(jnp.bfloat16)
    lane_group = (iota((ci, 128), 1) % 32 == iota((ci, 128), 0) // SIZE).astype(jnp.bfloat16)

    def split(a):
        high = a.astype(jnp.bfloat16).astype(jnp.float32)
        rest = a - high
        middle = rest.astype(jnp.bfloat16).astype(jnp.float32)
        low = rest - middle
        return jnp.concatenate([high, middle, low, jnp.zeros_like(a)], axis=0).astype(jnp.bfloat16)

    def gather(parts, zero_one):
        r = dot(parts, zero_one)
        return (r[0:8] + r[8:16]) + r[16:24]

    def frame_sums(j, v):
        lines[j] = jnp.sum(v, axis=0, keepdims=True)
        lines[2 + j] = jnp.sum(v * v, axis=0, keepdims=True)

    def own_stats(layer):
        stacked = jnp.concatenate(
            [lines[q] for q in range(4)] + [jnp.zeros((4, ci), jnp.float32)], axis=0
        )
        by_group = gather(split(stacked), lane_group)
        own = iota((8, 128), 0) == iota((8, 128), 1) // 32
        stats[layer, 0] = jnp.sum(jnp.where(own, by_group, 0.0), axis=0, keepdims=True)

    def send_stats(layer):
        def go(d, carry):
            pltpu.make_async_remote_copy(
                src_ref=stats.at[layer, 0], dst_ref=stats.at[layer, d],
                send_sem=ssend.at[layer], recv_sem=srecv.at[layer],
                device_id=peer(d), device_id_type=MESH,
            ).start()
            return carry

        lax.fori_loop(1, T, go, 0, unroll=True)

    def clip_stats(layer):
        stat_wait(layer, srecv)
        every = stats[layer]
        rows = []
        for f in range(4):
            inside = jnp.logical_and(frame >= starts[f], frame < starts[f] + counts[f])
            total = jnp.sum(jnp.where(inside, every, 0.0), axis=0)
            cells = jnp.maximum(counts[f], 1).astype(jnp.float32) * float(SIZE * CELLS)
            rows.append(total / jnp.full((1, 128), cells))
        parts = split(jnp.concatenate(rows + [jnp.zeros((4, 128), jnp.float32)], axis=0))
        mean = gather(parts, pick_sum)
        var = gather(parts, pick_sq) - mean * mean
        return mean, lax.rsqrt(var + EPS)

    column = iota((CELLS, ci), 0) % W

    def place(f, data, mean, scale, gamma, beta, slots):
        u = (data - mean[f : f + 1]) * (scale[f : f + 1] * gamma) + beta
        h = 0.5 * u * (1.0 + jnp.tanh(0.5 * u))
        before = jnp.where(column == 0, 0.0, pltpu.roll(h, 1, 0))
        after = jnp.where(column == W - 1, 0.0, pltpu.roll(h, CELLS - 1, 0))
        for kw, v in enumerate((before, h, after)):
            for kt, j in slots:
                if kt == 2:
                    kept = v
                else:
                    keep = jnp.full((CELLS, ci), starts[2 + j]) <= first + (j - 2 + kt)
                    kept = jnp.where(keep, v, 0.0)
                hs[kt, j, W : W + CELLS, kw * ci : (kw + 1) * ci] = kept.astype(jnp.bfloat16)

    def run_layer(layer, carry):
        mean, scale = clip_stats(layer)
        gamma, beta, bias = [par[3 * layer + q] for q in range(3)]
        for f, slots in ((2, [(2, 0), (1, 1)]), (3, [(2, 1)])):
            data = ybuf[layer, f - 2].astype(jnp.float32)
            place(f, data, mean, scale, gamma, beta, slots)
        for f, slots in ((0, [(0, 0)]), (1, [(1, 0), (0, 1)])):

            @pl.when(me > 0)
            def _():
                halo_copy(layer, f).wait_recv()

            data = halo[layer, f].astype(jnp.float32)
            place(f, data, mean, scale, gamma, beta, slots)

        def block(k, j, row, count):
            total = None
            for kt in range(3):
                pieces = [
                    hs[kt, j, pl.ds(pl.multiple_of(row + kh * W, W), count), :] for kh in range(3)
                ]
                if ci % 128 == 0:
                    weights = wbuf[layer, k, 9 * kt : 9 * kt + 9].reshape(9 * ci, ci)
                    terms = [dot(jnp.concatenate(pieces, axis=1), weights)]
                else:
                    terms = [
                        dot(piece, wbuf[layer, k, 9 * kt + 3 * kh : 9 * kt + 3 * kh + 3].reshape(3 * ci, ci))
                        for kh, piece in enumerate(pieces)
                    ]
                for term in terms:
                    total = term if total is None else total + term
            return total

        def early(i, carry):
            k = i // 2 + 1
            half = lax.rem(i, 2)

            @pl.when(half == 0)
            def _():
                w_copy(w1_ref, layer, k).wait()

            row = pl.multiple_of(half * HALF, HALF)
            psend[layer, k, 0, pl.ds(row, HALF), :] = block(k, 0, row, HALF).astype(jnp.bfloat16)
            part_copy(layer, k, half).start()
            return carry

        lax.fori_loop(0, 2 * (n - 1), early, 0)

        def late(i, carry):
            k = jnp.where(i < n, lax.rem(i + 1, n), 0)
            j = jnp.where(i < n, 1, 0)

            @pl.when(i == n - 1)
            def _():
                w_copy(w1_ref, layer, 0).wait()

            total = block(k, j, 0, CELLS)

            @pl.when(i < n - 1)
            def _():
                psend[layer, k, 1] = total.astype(jnp.bfloat16)
                part_copy(layer, k, 2).start()

            @pl.when(i >= n - 1)
            def _():
                acc[j] = total + bias

            return carry

        lax.fori_loop(0, n + 1, late, 0)
        for j in range(2):
            z = acc[j]
            for k in range(1, n):
                for piece in ((0, 1), (2,))[j]:
                    part_copy(layer, k, piece).wait_recv()
                z = z + precv[layer, k, j].astype(jnp.float32)
            y = z.astype(jnp.bfloat16)

            @pl.when(layer == 0)
            def _():
                ybuf[1, j] = y

            @pl.when(layer == 1)
            def _():
                turned = (z + ybuf[0, j].astype(jnp.float32)).T
                for q in range(2):
                    out_ref[pl.ds(2 * q + j, ci, stride=4), :] = turned[:, q * 128 : q * 128 + 128]

            @pl.when(jnp.logical_and(layer == 0, me < T - 1))
            def _():
                halo_copy(1, j).start()

            frame_sums(j, y.astype(jnp.float32))

        @pl.when(layer == 0)
        def _():
            own_stats(1)
            send_stats(1)

        return carry

    loads[0].wait()
    x_full[...] = x_half[...].astype(jnp.float32)
    for j in range(2):
        for q in range(2):
            turned = x_full[pl.ds(2 * q + j, ci, stride=4), :].T
            ybuf[0, j, q * 128 : q * 128 + 128, :] = turned.astype(jnp.bfloat16)
        frame_sums(j, ybuf[0, j].astype(jnp.float32))
    own_stats(0)
    pl.semaphore_wait(barrier, T - 1 + n - 1)
    send_stats(0)

    @pl.when(me < T - 1)
    def _():
        for j in range(2):
            halo_copy(0, j).start()

    hs[:, :, 0:W, :] = jnp.zeros((3, 2, W, 3 * ci), jnp.bfloat16)
    hs[:, :, W + CELLS :, :] = jnp.zeros((3, 2, W, 3 * ci), jnp.bfloat16)

    @pl.when(me == 0)
    def _():
        halo[...] = jnp.zeros_like(halo)

    first = 2 * me
    starts, counts = [], []
    for f in range(4):
        g = first - 2 + f
        begin = jnp.int32(0)
        count = jnp.int32(0)
        run = jnp.int32(0)
        for c in range(nclip):
            size = len_ref[c]
            inside = jnp.logical_and(run <= g, g < run + size)
            begin = jnp.where(inside, run, begin)
            count = jnp.where(inside, size, count)
            run = run + size
        starts.append(begin)
        counts.append(count)

    slot = iota((T, 1, 128), 0)
    frame = 2 * jnp.where(slot <= me, me - slot, me - slot + T) + (iota((T, 1, 128), 2) // 32) % 2
    for load in loads[1:]:
        load.wait()
    lax.fori_loop(0, 2, run_layer, 0)

    for layer in range(2):

        @pl.when(me < T - 1)
        def _():
            for j in range(2):
                halo_copy(layer, j).wait_send()

        stat_wait(layer, ssend)
        for k in range(1, n):
            for piece in range(3):
                part_copy(layer, k, piece).wait_send()


def lines_of(x):
    ci, frames, cells = x.shape
    return x.reshape(ci, frames, 2, 128).transpose(0, 2, 1, 3).reshape(4 * ci, 128)


def on_device(n, T, x, lengths, g1, b1, w1, c1, g2, b2, w2, c2):
    ci, frames, cells = x.shape
    wide = ci % 128 == 0
    if wide:
        w1, w2 = [w.transpose(1, 0, 2) for w in (w1, w2)]
    else:
        w1, w2 = [w.reshape(ci, 27, n, ci).transpose(2, 1, 0, 3) for w in (w1, w2)]
    params = [v.reshape(1, ci) for v in (g1, b1, c1, g2, b2, c2)]
    hbm = pl.BlockSpec(memory_space=pl.ANY)
    dma = pltpu.SemaphoreType.DMA
    cube = (2, CELLS, ci)
    out = pl.pallas_call(
        functools.partial(kernel, n, T, lengths.shape[0], wide),
        out_shape=jax.ShapeDtypeStruct((4 * ci, 128), jnp.float32),
        in_specs=[pl.BlockSpec(memory_space=pltpu.SMEM)] + [hbm] * 9,
        out_specs=pl.BlockSpec(memory_space=pltpu.VMEM),
        scratch_shapes=[
            pltpu.VMEM((2, n, 27, ci, ci), jnp.bfloat16),
            pltpu.VMEM((3, 2, PAD, 3 * ci), jnp.bfloat16),
            pltpu.VMEM((2,) + cube, jnp.bfloat16),
            pltpu.VMEM((2, T, 1, 128), jnp.float32),
            pltpu.VMEM((4, 1, ci), jnp.float32),
            pltpu.VMEM((2, n) + cube, jnp.bfloat16),
            pltpu.VMEM((2, n) + cube, jnp.bfloat16),
            pltpu.VMEM((2,) + cube, jnp.bfloat16),
            pltpu.VMEM(cube, jnp.float32),
            pltpu.VMEM((4 * ci, 128), jnp.bfloat16),
            pltpu.VMEM((4 * ci, 128), jnp.float32),
            pltpu.VMEM((6, 1, ci), jnp.float32),
            dma((2, n)),
            dma((7,)),
            dma((2, 2)),
            dma((2, 2)),
            dma((2,)),
            dma((2,)),
            dma((2, n, 3)),
            dma((2, n, 3)),
        ],
        compiler_params=pltpu.CompilerParams(
            collective_id=0, has_side_effects=True, vmem_limit_bytes=56 * 2**20
        ),
        cost_estimate=pl.CostEstimate(
            flops=4 * 27 * ci * C * 2 * CELLS, bytes_accessed=4 * 27 * ci * C, transcendentals=0
        ),
    )(lengths, lines_of(x), *params, w1, w2)
    return out.reshape(ci, 2, frames, 128).transpose(0, 2, 1, 3).reshape(ci, frames, cells)


def solution(mesh):
    n, T = mesh.shape["chan"], mesh.shape["tm"]
    c = P("chan")
    cube = P("chan", None, None)
    data = P("chan", "tm", None)
    return jax.shard_map(
        functools.partial(on_device, n, T),
        mesh=mesh,
        in_specs=(data, P(), c, c, cube, c, c, c, cube, c),
        out_specs=data,
        check_vma=False,
    )
```
